32 devices in a mesh: clips: 2 (over x), ulysses: 4 (over y, core), tm: 4 (over z).
Axes of the slice: x: 2, y: 2, z: 4, core: 2. Of those that a mesh axis runs over, the one named last changes fastest.
Arguments:
- queries: bfloat16 [4096, 3072], P(('clips', 'tm', 'ulysses')), parts along dimension 0, may hold values from -90 to 90
- key_vectors: bfloat16 [4096, 3072], P(('clips', 'tm', 'ulysses')), parts along dimension 0, may hold values from -5 to 5
- value_vectors: bfloat16 [4096, 3072], P(('clips', 'tm', 'ulysses')), parts along dimension 0, may hold values from -6 to 6
- grad_out: bfloat16 [4096, 3072], P(('clips', 'tm', 'ulysses')), parts along dimension 0, may hold values from -6 to 6
- key_tiles: int32 [64, 3], P('clips'), parts along dimension 0, may hold values from 0 to 31, as said below
- tile_counts: int32 [64], P('clips'), parts along dimension 0, may hold values from 2 to 3, as said below
Outputs:
- attended: bfloat16 [4096, 3072], P(('clips', 'tm', 'ulysses')), parts along dimension 0
- grad_queries: bfloat16 [4096, 3072], P(('clips', 'tm', 'ulysses')), parts along dimension 0
- grad_keys: bfloat16 [4096, 3072], P(('clips', 'tm', 'ulysses')), parts along dimension 0
- grad_values: bfloat16 [4096, 3072], P(('clips', 'tm', 'ulysses')), parts along dimension 0
The draws below stay inside these ranges and needn't reach their ends.
There are 2 independent parts, one for each index of `clips`. The reference program is written for one: setup_inputs(seed, part) draws one part's arguments, and reference() takes and returns one part's arrays. A program takes and returns all parts, laid end to end along the dimension named above; each array names one. Nothing has to cross between parts.
Inputs may be any that keep to these rules, and one draw needn't show every extreme that they name: `key_tiles`: row i holds distinct tiles of the frame of query tile i and of the frames just before and after it; entry 0 is tile i itself, then one tile of the frame before and one of the frame after where those frames exist, then the rest in no fixed order; entries from position tile_counts[i] on repeat entry 0. The query tiles of one frame together list exactly 1 tiles of the frame before it and exactly 1 of the frame after it, where those frames exist. `tile_counts`: the first 1 query tiles of every frame have count 3.
All inputs are finite; a program needn't handle non-finite values.
Results may differ from the reference program's by a relative error of at most 0.022.
Values may be sent and summed in bfloat16 or wider, within the bound.
No kernel may reach another device: no remote copies, remote signals or barrier semaphores. Data moves between devices by JAX's collectives and lax.ppermute only.
A program may use at most 192 MiB of HBM per device.

```python
import jax
import jax.numpy as jnp
from jax import lax

HEADS = 48
HEAD_DIM = 64
TILE = 64
FRAMES_SLAB = 2
FRAME_TILES = 4
FRAMES = 8
TOKENS = 2048
Q_TILES = 32
REMOTE = 1
MAXK = 3
N_TM = 4


def draw_pair(key):
    base_key = jax.random.fold_in(key, 101)
    query_key, vector_key = jax.random.split(base_key, 2)
    row_width = HEADS * HEAD_DIM
    query_draw = jnp.clip(jax.random.normal(query_key, (TOKENS, row_width), jnp.float32), -4.0, 4.0)
    key_draw = jnp.clip(jax.random.normal(vector_key, (TOKENS, row_width), jnp.float32), -4.0, 4.0)
    return (query_draw.astype(jnp.bfloat16), key_draw.astype(jnp.bfloat16))


def draw_queries(key, part):
    return draw_pair(key)[0]


def draw_key_vectors(key, part):
    return draw_pair(key)[1]


def draw_lists(key):
    base_key = jax.random.fold_in(key, 202)
    earlier_key, later_key, rank_key, count_key = jax.random.split(base_key, 4)
    frame_tiles = FRAME_TILES
    remote = REMOTE
    list_width = MAXK
    tile_total = Q_TILES
    frame_total = FRAMES
    candidate_total = frame_tiles + 2 * remote

    def first_picks(sub_key):
        return jax.random.permutation(sub_key, frame_tiles)[:remote].astype(jnp.int32)
    earlier_sets = jax.vmap(first_picks)(jax.random.split(earlier_key, frame_total))
    later_sets = jax.vmap(first_picks)(jax.random.split(later_key, frame_total))
    tile_index = jnp.arange(tile_total, dtype=jnp.int32)
    frame_of = tile_index // frame_tiles
    inner_index = tile_index % frame_tiles
    spot_index = jnp.arange(frame_tiles, dtype=jnp.int32)
    local_tiles = frame_of[:, None] * frame_tiles + spot_index[None, :]
    earlier_tiles = (frame_of[:, None] - 1) * frame_tiles + earlier_sets[frame_of]
    later_tiles = (frame_of[:, None] + 1) * frame_tiles + later_sets[frame_of]
    candidates = jnp.concatenate([local_tiles, earlier_tiles, later_tiles], axis=1)
    picked = jnp.arange(remote, dtype=jnp.int32)[None, :] == (inner_index % remote)[:, None]
    has_earlier = (frame_of > 0)[:, None]
    has_later = (frame_of < frame_total - 1)[:, None]
    priority_local = jnp.where(spot_index[None, :] == inner_index[:, None], 0, 3)
    priority_earlier = jnp.where(has_earlier, jnp.where(picked, 1, 3), 4)
    priority_later = jnp.where(has_later, jnp.where(picked, 2, 3), 4)
    priority = jnp.concatenate([priority_local, priority_earlier, priority_later], axis=1).astype(jnp.int32)

    def random_rank(sub_key):
        return jax.random.permutation(sub_key, candidate_total).astype(jnp.int32)
    ranks = jax.vmap(random_rank)(jax.random.split(rank_key, tile_total))
    ordering = jnp.argsort(priority * candidate_total + ranks, axis=1)
    chosen = jnp.take_along_axis(candidates, ordering, axis=1)[:, :list_width]
    counts = jax.random.randint(count_key, (tile_total,), list_width // 2 + 1, list_width + 1)
    counts = jnp.where(inner_index < remote, list_width, counts).astype(jnp.int32)
    slot_index = jnp.arange(list_width, dtype=jnp.int32)
    chosen = jnp.where(slot_index[None, :] < counts[:, None], chosen, chosen[:, :1])
    return (chosen.astype(jnp.int32), counts)


def draw_key_tiles(key, part):
    return draw_lists(key)[0]


def draw_tile_counts(key, part):
    return draw_lists(key)[1]


def block_scale(rng, extent, pieces, smallest, largest):
    def one(dim, shards_of):
        steps = jax.random.uniform(jax.random.fold_in(jax.random.fold_in(rng, 6), dim), (shards_of,), jnp.float32, smallest / len(pieces), largest / len(pieces))
        return jnp.repeat(jnp.exp(steps), extent[dim] // shards_of).reshape((-1,) + (1,) * (len(extent) - dim - 1))

    gain = one(*pieces[0])
    for cut in pieces[1:]:
        gain = gain * one(*cut)
    return gain


def gaussian(key, shape, scale, reach, cuts=(), kind=jnp.bfloat16):
    result = jax.random.normal(key, shape, jnp.float32) * scale
    if len(cuts) > 0:
        result = block_scale(key, shape, cuts, -0.22, 0.18) * result
    return jnp.clip(result, min=-reach, max=reach).astype(kind)


def setup_inputs(seed: int = 0, part: int = 0) -> dict:
    arg_keys = jax.random.split(jax.random.key(seed), 7)
    part_splits = jax.random.split(jax.random.fold_in(arg_keys[6], part), 7)
    return {
        "queries": draw_queries(jax.random.fold_in(jax.random.fold_in(arg_keys[6], part), 71), part),
        "key_vectors": draw_key_vectors(jax.random.fold_in(jax.random.fold_in(arg_keys[6], part), 71), part),
        "value_vectors": gaussian(part_splits[2], (TOKENS, HEADS * HEAD_DIM), 1.0, 6.0, ((0, 16),)),
        "grad_out": gaussian(part_splits[3], (TOKENS, HEADS * HEAD_DIM), 1.0, 6.0, ((0, 16),)),
        "key_tiles": draw_key_tiles(jax.random.fold_in(jax.random.fold_in(arg_keys[6], part), 71), part),
        "tile_counts": draw_tile_counts(jax.random.fold_in(jax.random.fold_in(arg_keys[6], part), 71), part),
    }


def attend(query_rows, key_rows, value_rows, grad_rows, live_keys, score_scale):
    best = lax.Precision.HIGHEST
    query_full = query_rows.astype(jnp.float32)
    key_full = key_rows.astype(jnp.float32)
    value_full = value_rows.astype(jnp.float32)
    grad_full = grad_rows.astype(jnp.float32)
    scores = jnp.einsum("bqhd,bkhd->bhqk", query_full, key_full, precision=best) * score_scale
    key_mask = live_keys[:, None, None, :]
    scores = jnp.where(key_mask, scores, -jnp.inf)
    row_peak = jnp.max(scores, axis=-1, keepdims=True)
    expo_terms = jnp.where(key_mask, jnp.exp(scores - row_peak), 0.0)
    prob_full = expo_terms / jnp.sum(expo_terms, axis=-1, keepdims=True)
    prob_low = lax.optimization_barrier(prob_full.astype(jnp.bfloat16)).astype(jnp.float32)
    out_rows = jnp.einsum("bhqk,bkhd->bqhd", prob_low, value_full, precision=best).astype(jnp.bfloat16)
    row_delta = jnp.sum(grad_full * out_rows.astype(jnp.float32), axis=-1)
    grad_probs = jnp.einsum("bqhd,bkhd->bhqk", grad_full, value_full, precision=best)
    grad_scores = prob_full * (grad_probs - jnp.transpose(row_delta, (0, 2, 1))[..., None])
    grad_low = lax.optimization_barrier(grad_scores.astype(jnp.bfloat16)).astype(jnp.float32)
    grad_query_rows = (jnp.einsum("bhqk,bkhd->bqhd", grad_low, key_full, precision=best) * score_scale).astype(jnp.bfloat16)
    key_part = jnp.einsum("bhqk,bqhd->bkhd", grad_low, query_full, precision=best) * score_scale
    value_part = jnp.einsum("bhqk,bqhd->bkhd", prob_low, grad_full, precision=best)
    return out_rows, grad_query_rows, key_part, value_part


def reference(queries, key_vectors, value_vectors, grad_out, key_tiles, tile_counts):
    own_tiles = FRAMES_SLAB * FRAME_TILES
    row_width = HEADS * HEAD_DIM
    tile_shape = (Q_TILES, TILE, HEADS, HEAD_DIM)
    query_tiled = queries.reshape(tile_shape)
    key_tiled = key_vectors.reshape(tile_shape)
    value_tiled = value_vectors.reshape(tile_shape)
    grad_tiled = grad_out.reshape(tile_shape)
    score_scale = HEAD_DIM ** -0.5

    def one_slab(slab_index):
        first_tile = (slab_index * own_tiles).astype(jnp.int32)
        tile_lists = lax.dynamic_slice(key_tiles, (first_tile, jnp.int32(0)), (own_tiles, MAXK))
        counts = lax.dynamic_slice(tile_counts, (first_tile,), (own_tiles,))
        query_block = lax.dynamic_slice_in_dim(query_tiled, first_tile, own_tiles, 0)
        grad_block = lax.dynamic_slice_in_dim(grad_tiled, first_tile, own_tiles, 0)
        key_block = key_tiled[tile_lists].reshape(own_tiles, MAXK * TILE, HEADS, HEAD_DIM)
        value_block = value_tiled[tile_lists].reshape(own_tiles, MAXK * TILE, HEADS, HEAD_DIM)
        live_keys = jnp.repeat(jnp.arange(MAXK, dtype=jnp.int32)[None, :] < counts[:, None], TILE, axis=1)
        out_rows, grad_query_rows, key_part, value_part = attend(query_block, key_block, value_block, grad_block, live_keys, score_scale)
        slot_index = (tile_lists - first_tile + FRAME_TILES).astype(jnp.int32).reshape(-1)
        ext_shape = (own_tiles + 2 * FRAME_TILES, TILE, HEADS, HEAD_DIM)
        flat_shape = (own_tiles * MAXK, TILE, HEADS, HEAD_DIM)
        key_sum = jnp.zeros(ext_shape, jnp.float32).at[slot_index].add(key_part.reshape(flat_shape))
        value_sum = jnp.zeros(ext_shape, jnp.float32).at[slot_index].add(value_part.reshape(flat_shape))
        upper_start = FRAME_TILES + own_tiles
        return (out_rows, grad_query_rows,
                key_sum[FRAME_TILES:upper_start], value_sum[FRAME_TILES:upper_start],
                key_sum[:FRAME_TILES].astype(jnp.bfloat16), value_sum[:FRAME_TILES].astype(jnp.bfloat16),
                key_sum[upper_start:].astype(jnp.bfloat16), value_sum[upper_start:].astype(jnp.bfloat16))

    results = lax.map(one_slab, jnp.arange(N_TM, dtype=jnp.int32))
    out_all, grad_query_all, key_own, value_own, key_low, value_low, key_high, value_high = results

    def combine(own_sum, lower_border, upper_border):
        lower_border = lax.optimization_barrier(lower_border).astype(jnp.float32)
        upper_border = lax.optimization_barrier(upper_border).astype(jnp.float32)
        from_above = jnp.concatenate([lower_border[1:], jnp.zeros_like(lower_border[:1])], axis=0)
        from_below = jnp.concatenate([jnp.zeros_like(upper_border[:1]), upper_border[:-1]], axis=0)
        own_sum = own_sum.at[:, own_tiles - FRAME_TILES:].add(from_above)
        own_sum = own_sum.at[:, :FRAME_TILES].add(from_below)
        return own_sum.astype(jnp.bfloat16).reshape(TOKENS, row_width)

    attended = out_all.reshape(TOKENS, row_width)
    grad_queries = grad_query_all.reshape(TOKENS, row_width)
    grad_keys = combine(key_own, key_low, key_high)
    grad_values = combine(value_own, value_low, value_high)
    return attended, grad_queries, grad_keys, grad_values
```

```python
import functools

import jax
import jax.numpy as jnp
from jax import lax
from jax.experimental import pallas as pl
from jax.experimental.pallas import tpu as pltpu
from jax.sharding import PartitionSpec as P

HEAD_DIM = 64
TILE = 64
FRAMES_SLAB = 2
PAIR = 2 * HEAD_DIM
BLOCK = 32
NEG = -1e30
VMEM_LIMIT = 24 * 1024 * 1024


class Plan:
    def __init__(self, rows, width, list_width):
        self.rows, self.width, self.list_width = rows, width, list_width
        self.slab = lax.axis_size("ulysses")
        self.slabs = lax.axis_size("tm")
        self.members = self.slab // FRAMES_SLAB
        self.frames = self.slabs * FRAMES_SLAB
        self.cols = width // self.members
        self.pairs = self.cols // PAIR
        self.device_tiles = rows // TILE
        self.frame_tiles = self.members * self.device_tiles
        self.remote = max(1, self.frame_tiles // 8)
        self.ext_tiles = self.frame_tiles + 2 * self.remote
        chunks = 2 if self.pairs % 2 == 0 else 1
        self.chunk_pairs = [self.pairs // chunks] * chunks
        self.span = 2 if self.chunk_pairs[0] % 2 == 0 else 1
        self.lanes = self.span * PAIR
        self.blocks = [count // self.span for count in self.chunk_pairs]
        self.unrolled = self.blocks[0] if self.frame_tiles <= 4 else 1
        self.whole_pieces = self.members == 2
        self.chunk_starts = [sum(self.chunk_pairs[:i]) for i in range(chunks)]

    def device(self, frame, member):
        place = frame % FRAMES_SLAB * self.members + member
        return place * self.slabs + frame // FRAMES_SLAB

    def member_perm(self, shift):
        return [
            (self.device(f, c), self.device(f, (c + shift) % self.members))
            for f in range(self.frames)
            for c in range(self.members)
        ]

    def frame_perm(self, far):
        pairs = [(f, partner(f, far)) for f in range(self.frames)]
        return [
            (self.device(f, c), self.device(other, c))
            for f, other in pairs
            if 0 <= other < self.frames
            for c in range(self.members)
        ]


def partner(frame, far):
    odd = frame % 2
    return frame - 1 + 2 * odd if far else frame + 1 - 2 * odd


def position(plan):
    place = lax.axis_index("ulysses")
    return lax.axis_index("tm") * FRAMES_SLAB + place // plan.members, place % plan.members


def piece_start(plan, me, offset):
    return pl.multiple_of(me * plan.cols + offset, PAIR) if plan.whole_pieces else offset


def listed(plan, lists_ref, counts_ref, reader, source):
    tiles = plan.frame_tiles
    row_start = jnp.clip(reader, 0, plan.frames - 1) * tiles
    base = source * tiles
    if plan.remote == 1:
        best = jnp.int32(0)
        for t in range(tiles):
            for j in range(plan.list_width):
                local = lists_ref[j, row_start + t] - base
                inside = (local >= 0) & (local < tiles) & (j < counts_ref[row_start + t])
                best = jnp.where(inside, local, best)
        return [best]

    def candidate(c, state):
        def row(t, found):
            for j in range(plan.list_width):
                hit = (lists_ref[j, row_start + t] == base + c) & (j < counts_ref[row_start + t])
                found = jnp.where(hit, 1, found)
            return found

        found = lax.fori_loop(0, tiles, row, jnp.int32(0))
        seen, picks = state
        picks = tuple(jnp.where((found == 1) & (seen == i), c, pick) for i, pick in enumerate(picks))
        return seen + found, picks

    start = (jnp.int32(0), tuple(jnp.int32(0) for _ in range(plan.remote)))
    return list(lax.fori_loop(0, tiles, candidate, start)[1])


def split_kernel(plan, *refs):
    count = (len(refs) - 1) // plan.members
    sources, outs, sem = refs[:count], refs[count:-1], refs[-1]
    _, me = position(plan)
    copies = []
    for r in range(1, plan.members):
        columns = pl.ds(pl.multiple_of((me + r) % plan.members * plan.cols, PAIR), plan.cols)
        for a, source in enumerate(sources):
            for row in range(0, plan.rows, BLOCK):
                rows = pl.ds(row, BLOCK)
                slot = len(copies)
                copies.append(
                    pltpu.make_async_copy(source.at[rows, columns], outs[(r - 1) * count + a].at[rows, :], sem.at[slot])
                )
    for copy in copies:
        copy.start()
    for copy in copies:
        copy.wait()


def slice_kernel(plan, after, *refs):
    refs = refs[after:]
    count = len(refs) // plan.members
    _, me = position(plan)
    for r in range(1, plan.members):
        columns = pl.ds(pl.multiple_of((me + r) % plan.members * plan.cols, PAIR), plan.cols)
        for a in range(count):
            refs[r * count + a][...] = refs[a][:, columns]


def pick_kernel(plan, g, lists_ref, counts_ref, *refs):
    members = plan.members
    own = refs[:2]
    pieces = refs[2 : 2 * members]
    outs = refs[-2:]
    frame, me = position(plan)
    cols = plan.chunk_pairs[g] * PAIR
    offset = plan.chunk_starts[g] * PAIR
    for far in range(2):
        picks = listed(plan, lists_ref, counts_ref, partner(frame, far), frame)
        for j, pick in enumerate(picks):
            owner = pick // plan.device_tiles
            row = pl.multiple_of(pick % plan.device_tiles * TILE, TILE)
            place = (me + members - owner) % members

            @pl.when(place == 0)
            def _():
                start = pl.multiple_of(me * plan.cols + offset, PAIR)
                for a in range(2):
                    outs[far][a, j] = own[a][pl.ds(row, TILE), pl.ds(start, cols)]

            for r in range(1, members):

                @pl.when(place == r)
                def _():
                    for a in range(2):
                        piece = pieces[(r - 1) * 2 + a]
                        outs[far][a, j] = piece[pl.ds(row, TILE), pl.ds(piece_start(plan, me, offset), cols)]


def attend_kernel(plan, g, lists_ref, counts_ref, *refs):
    members, tiles, remote, width = plan.members, plan.frame_tiles, plan.remote, plan.list_width
    per = plan.device_tiles
    others = members - 1
    own = refs[:4]
    key_value = refs[4 : 4 + 2 * others]
    query_grad = refs[4 + 2 * others : 4 + 4 * others]
    borders = refs[4 + 4 * others : 6 + 4 * others]
    rest = refs[6 + 4 * others :]
    earlier, rest = rest[: g * members], rest[g * members :]
    outs, parts = rest[:members], rest[members : members + 2]
    k_s, v_s, dk_s, dv_s, slots = rest[members + 2 :]
    last = g == len(plan.chunk_pairs) - 1
    for c in range(g if last else 0):
        done = pl.ds(plan.chunk_starts[c] * PAIR, plan.chunk_pairs[c] * PAIR)
        for r in range(members):
            outs[r][:, :, done] = earlier[c * members + r][...]
    frame, me = position(plan)
    partners = [partner(frame, far) for far in range(2)]
    known = [listed(plan, lists_ref, counts_ref, frame, other) for other in partners]
    live = []
    for t in range(tiles):
        row = frame * tiles + (me + members - t // per) % members * per + t % per
        live.append(counts_ref[row])
        for j in range(width):
            tile = lists_ref[j, row]
            local = tile - frame * tiles
            slot = (me + members - local // per) % members * per + local % per
            for far in range(2):
                local = tile - partners[far] * tiles
                rank = jnp.int32(0)
                for i in range(1, remote):
                    rank = jnp.where(local == known[far][i], i, rank)
                inside = (local >= 0) & (local < tiles)
                slot = jnp.where(inside, tiles + far * remote + rank, slot)
            slots[t, j] = slot

    lanes, heads = plan.lanes, plan.lanes // HEAD_DIM
    head_of = lax.broadcasted_iota(jnp.int32, (TILE, lanes), 1) // HEAD_DIM
    first = lax.broadcasted_iota(jnp.int32, (TILE, PAIR), 1) < HEAD_DIM
    scale = HEAD_DIM ** (-0.5)
    natural = (((1,), (0,)), ((), ()))
    inner = (((1,), (1,)), ((), ()))
    outer = (((0,), (0,)), ((), ()))

    def dot(left, right, dims):
        return lax.dot_general(left, right, dims, preferred_element_type=jnp.float32)

    def apart(rows):
        zero = jnp.zeros_like(rows)
        return jnp.concatenate([jnp.where(head_of == h, rows, zero) for h in range(heads)], axis=0)

    def together(terms, rows):
        pairs = []
        for s in range(plan.span):
            columns = slice(s * PAIR, (s + 1) * PAIR)
            both = dot(terms[:, columns], rows[:, columns], outer)
            pairs.append(jnp.where(first, both[:TILE], both[TILE:]))
        return jnp.concatenate(pairs, axis=1)

    def spans(p):
        offset = p * lanes
        start = plan.chunk_starts[g] * PAIR + offset
        if not isinstance(p, int):
            offset, start = pl.multiple_of(offset, lanes), pl.multiple_of(start, PAIR)
        here = pl.ds(pl.multiple_of(me * plan.cols + start, PAIR), lanes)
        there = pl.ds(piece_start(plan, me, start), lanes)
        span = pl.ds(offset, lanes)
        cut = pl.ds(start, lanes)
        return here, there, cut, span, cut if last else span

    def prepare(p, b):
        here, there, _, span, _ = spans(p)
        for a, scratch in enumerate((k_s, v_s)):
            for i in range(per):
                rows = pl.ds(i * TILE, TILE)
                scratch[b, i] = own[1 + a][rows, here]
                for r in range(1, members):
                    scratch[b, r * per + i] = key_value[(r - 1) * 2 + a][rows, there]
            for far in range(2):
                for i in range(remote):
                    scratch[b, tiles + far * remote + i] = borders[far][a, i, :, span]
        dk_s[b] = jnp.zeros(dk_s.shape[1:], dk_s.dtype)
        dv_s[b] = jnp.zeros(dv_s.shape[1:], dv_s.dtype)

    def first_products(p, b, t):
        here, _, cut, _, _ = spans(p)

        def load(a):
            rows = pl.ds(t % per * TILE, TILE)
            if t < per:
                return own[a][rows, here]
            return query_grad[(t // per - 1) * 2 + a // 3][rows, cut]

        at = [slots[t, j] for j in range(width)]
        queries = apart(load(0) * jnp.bfloat16(scale))
        grads = apart(load(3))
        keys = jnp.concatenate([k_s[b, s] for s in at], axis=0)
        values = jnp.concatenate([v_s[b, s] for s in at], axis=0)
        return at, queries, grads, keys, values, dot(keys, queries, inner), dot(values, grads, inner)

    def softmax(t, scores, grad_probs):
        masked = jnp.concatenate(
            [jnp.where(j < live[t], scores[j * TILE : (j + 1) * TILE], NEG) for j in range(width)], axis=0
        )
        terms = jnp.exp(masked - jnp.max(masked, axis=0, keepdims=True))
        probs = terms * (1.0 / jnp.sum(terms, axis=0, keepdims=True))
        delta = jnp.sum(probs * grad_probs, axis=0, keepdims=True)
        return probs.astype(jnp.bfloat16), (probs * (grad_probs - delta)).astype(jnp.bfloat16)

    def second_products(p, b, t, at, queries, grads, keys, values, probs_low, grad_low):
        result = spans(p)[-1]
        rows = pl.ds(t % per * TILE, TILE)
        out = outs[t // per]
        out[0, rows, result] = together(probs_low, values).astype(jnp.bfloat16)
        out[1, rows, result] = (together(grad_low, keys) * scale).astype(jnp.bfloat16)
        key_part = dot(grad_low, queries, natural)
        value_part = dot(probs_low, grads, natural)
        for j, s in enumerate(at):
            dk_s[b, s] += key_part[j * TILE : (j + 1) * TILE]
            dv_s[b, s] += value_part[j * TILE : (j + 1) * TILE]

    def finish(p, b):
        _, _, _, span, result = spans(p)
        for a, scratch in enumerate((dk_s, dv_s)):
            for t in range(tiles):
                rows = pl.ds(t % per * TILE, TILE)
                outs[t // per][2 + a, rows, result] = scratch[b, t].astype(jnp.bfloat16)
            for far in range(2):
                for i in range(remote):
                    parts[far][a, i, :, span] = scratch[b, tiles + far * remote + i].astype(jnp.bfloat16)

    def some_blocks(places):
        steps = [(p, b, t) for b, p in enumerate(places) for t in range(tiles)]
        products, weights = {}, {}
        for n in range(len(steps) + 2):
            if n < len(steps):
                p, b, t = steps[n]
                if t == 0:
                    prepare(p, b)
                products[n] = first_products(p, b, t)
            if 0 <= n - 1 < len(steps):
                weights[n - 1] = softmax(steps[n - 1][2], *products[n - 1][5:])
            if 0 <= n - 2:
                p, b, t = steps[n - 2]
                second_products(p, b, t, *products.pop(n - 2)[:5], *weights.pop(n - 2))
                if t == tiles - 1:
                    finish(p, b)

    if plan.unrolled == plan.blocks[g]:
        some_blocks(range(plan.blocks[g]))
    else:
        lax.fori_loop(0, plan.blocks[g], lambda p, carry: (some_blocks([p]), carry)[1], 0)


def write_out(scratch, outs, sem, fill):
    copies = []
    for a in range(2):
        for i in range(outs[a].shape[0] // TILE):
            rows = pl.ds(i * TILE, TILE)
            fill(a, i, rows)
            slot = len(copies)
            copies.append(pltpu.make_async_copy(scratch.at[a, rows, :], outs[a].at[rows, :], sem.at[slot]))
            copies[-1].start()
    for copy in copies:
        copy.wait()


def join_kernel(plan, *refs):
    members, outs, scratch, sem = plan.members, refs[-4:-2], refs[-2], refs[-1]
    _, me = position(plan)

    def fill(a, i, rows):
        for r in range(members):
            start = pl.multiple_of((me + r) % members * plan.cols, PAIR)
            scratch[a, rows, pl.ds(start, plan.cols)] = refs[r][a, rows, :]

    write_out(scratch, outs, sem, fill)


def add_kernel(plan, lists_ref, counts_ref, *refs):
    members, outs, scratch, sem = plan.members, refs[-4:-2], refs[-2], refs[-1]
    pieces, borders = refs[:members], refs[members:-4]
    frame, me = position(plan)
    partners = [partner(frame, far) for far in range(2)]
    picks = [listed(plan, lists_ref, counts_ref, other, frame) for other in partners]

    def fill(a, i, rows):
        hits = []
        for far in range(2):
            exists = (partners[far] >= 0) & (partners[far] < plan.frames)
            for j, pick in enumerate(picks[far]):
                hits.append((far, j, exists & (pick == me * plan.device_tiles + i)))
        for r in range(members):
            start = pl.multiple_of((me + r) % members * plan.cols, PAIR)
            scratch[a, rows, pl.ds(start, plan.cols)] = pieces[r][2 + a, rows, :]

        @pl.when(functools.reduce(lambda x, y: x | y, [hit for _, _, hit in hits]))
        def _():
            for g, count in enumerate(plan.chunk_pairs):
                for r in range(members):
                    columns = pl.ds(plan.chunk_starts[g] * PAIR, count * PAIR)
                    start = (me + r) % members * plan.cols + plan.chunk_starts[g] * PAIR
                    total = pieces[r][2 + a, rows, columns].astype(jnp.float32)
                    for far, j, hit in hits:
                        border = borders[(g * members + r) * 2 + far]
                        total += jnp.where(hit, border[a, j].astype(jnp.float32), 0.0)
                    span = pl.ds(pl.multiple_of(start, PAIR), count * PAIR)
                    scratch[a, rows, span] = total.astype(jnp.bfloat16)

    write_out(scratch, outs, sem, fill)


def per_device(queries, key_vectors, value_vectors, grad_out, key_tiles, tile_counts):
    rows, width = queries.shape
    plan = Plan(rows, width, key_tiles.shape[1])
    members, remote, chunks = plan.members, plan.remote, len(plan.chunk_pairs)
    axes = ("ulysses", "tm")
    lists = key_tiles.T
    low = jnp.bfloat16
    scalars = pl.BlockSpec(memory_space=pltpu.SMEM)
    whole = pl.BlockSpec(memory_space=pltpu.VMEM)
    anywhere = pl.BlockSpec(memory_space=pl.ANY)
    shape = jax.ShapeDtypeStruct
    params = pltpu.CompilerParams(vmem_limit_bytes=VMEM_LIMIT)

    def cost(moved, flops=0, terms=0):
        return pl.CostEstimate(flops=flops, bytes_accessed=moved, transcendentals=terms)

    def exchange(name, whole_rows, after, *sources):
        if plan.whole_pieces and whole_rows:
            return [lax.ppermute(x, axes, plan.member_perm(1)) for x in sources]
        places = (members - 1) * len(sources) * (rows // BLOCK)
        direct = not plan.whole_pieces
        after = [] if direct else after
        kernel = functools.partial(split_kernel, plan) if direct else functools.partial(slice_kernel, plan, len(after))
        sends = pl.pallas_call(
            kernel,
            out_shape=[shape((rows, plan.cols), low)] * (members - 1) * len(sources),
            in_specs=[anywhere] * len(after) + [anywhere if direct else whole] * len(sources),
            out_specs=[whole] * (members - 1) * len(sources),
            scratch_shapes=[pltpu.SemaphoreType.DMA((places,))] if direct else [],
            compiler_params=params,
            cost_estimate=cost(4 * len(sources) * rows * width),
            name=name,
        )(*after, *[pltpu.with_memory_space_constraint(x, pltpu.HBM) if direct else x for x in sources])
        each = len(sources)
        return [lax.ppermute(x, axes, plan.member_perm(1 + n // each)) for n, x in enumerate(sends)]

    key_value = exchange("split_kv", True, [], key_vectors, value_vectors)

    def hold_kernel(after, *refs):
        refs = refs[after:]
        for source, out in zip(refs[: len(refs) // 2], refs[len(refs) // 2 :], strict=True):
            out[...] = source[...]

    def hold(name, after, *sources):
        return pl.pallas_call(
            functools.partial(hold_kernel, len(after)),
            out_shape=[shape(x.shape, low) for x in sources],
            in_specs=[anywhere] * len(after) + [whole] * len(sources),
            out_specs=[whole] * len(sources),
            compiler_params=params,
            cost_estimate=cost(4 * sum(x.size for x in sources)),
            name=name,
        )(*after, *sources)

    arrived = []
    for g, count in enumerate(plan.chunk_pairs):
        picked = pl.pallas_call(
            functools.partial(pick_kernel, plan, g),
            out_shape=[shape((2, remote, TILE, count * PAIR), low)] * 2,
            in_specs=[scalars] * 2 + [whole] * (2 * members),
            out_specs=[whole] * 2,
            compiler_params=params,
            cost_estimate=cost(16 * remote * TILE * count * PAIR),
            name=f"pick_{g}",
        )(lists, tile_counts, key_vectors, value_vectors, *key_value)
        near, far = picked
        if g > 0:
            [near] = hold(f"hold_near_{g}", [arrived[-1][0]], near)
        arrived.append([lax.ppermute(x, axes, plan.frame_perm(i)) for i, x in enumerate((near, far))])
    query_grad = exchange("split_qg", False, [], queries, grad_out)

    def home(sent, r):
        return lax.ppermute(sent, axes, plan.member_perm(members - r))

    earlier, border_terms, nears, fars = [], [], [], []
    for g, count in enumerate(plan.chunk_pairs):
        cols = count * PAIR
        wide = plan.cols if g == chunks - 1 else cols
        scores = plan.frame_tiles * plan.list_width * TILE * 2 * TILE * count
        outs = pl.pallas_call(
            functools.partial(attend_kernel, plan, g),
            out_shape=[shape((4, rows, wide), low)] * members + [shape((2, remote, TILE, cols), low)] * 2,
            in_specs=[scalars] * 2 + [whole] * (4 + 4 * (members - 1) + 2 + len(earlier)),
            out_specs=[whole] * (members + 2),
            scratch_shapes=[
                pltpu.VMEM((plan.unrolled, plan.ext_tiles, TILE, plan.lanes), low),
                pltpu.VMEM((plan.unrolled, plan.ext_tiles, TILE, plan.lanes), low),
                pltpu.VMEM((plan.unrolled, plan.ext_tiles, TILE, plan.lanes), jnp.float32),
                pltpu.VMEM((plan.unrolled, plan.ext_tiles, TILE, plan.lanes), jnp.float32),
                pltpu.SMEM((plan.frame_tiles, plan.list_width), jnp.int32),
            ],
            compiler_params=params,
            cost_estimate=cost(16 * members * rows * cols, 12 * scores * PAIR, scores),
            name=f"attend_{g}",
        )(
            lists, tile_counts, queries, key_vectors, value_vectors, grad_out,
            *key_value, *query_grad, *arrived[g], *earlier,
        )
        parts = list(outs[members:])
        earlier += outs[:members]
        if g > 0:
            held = hold(f"hold_far_{g}", [nears[-1], fars[-1]], parts[1], *earlier[1 - members :])
            parts[1], earlier[1 - members :] = held[0], held[1:]
        nears.append(lax.ppermute(parts[0], axes, plan.frame_perm(0)))
        fars.append(lax.ppermute(parts[1], axes, plan.frame_perm(1)))
    for near, far in zip(nears, fars, strict=True):
        border_terms += [near, far]
        for r in range(1, members):
            border_terms += [home(near, r), home(far, r)]
    pieces = [earlier[-members], *[home(earlier[r - members], r) for r in range(1, members)]]

    attended, grad_queries = pl.pallas_call(
        functools.partial(join_kernel, plan),
        out_shape=[shape((rows, width), low)] * 2,
        in_specs=[whole] * members,
        out_specs=[pl.BlockSpec(memory_space=pltpu.HBM)] * 2,
        scratch_shapes=[pltpu.VMEM((2, rows, width), low), pltpu.SemaphoreType.DMA((2 * plan.device_tiles,))],
        compiler_params=params,
        cost_estimate=cost(8 * rows * width),
        name="join",
    )(*pieces)
    grad_keys, grad_values = pl.pallas_call(
        functools.partial(add_kernel, plan),
        out_shape=[shape((rows, width), low)] * 2,
        in_specs=[scalars] * 2 + [whole] * (members + len(border_terms)),
        out_specs=[pl.BlockSpec(memory_space=pltpu.HBM)] * 2,
        scratch_shapes=[pltpu.VMEM((2, rows, width), low), pltpu.SemaphoreType.DMA((2 * plan.device_tiles,))],
        compiler_params=params,
        cost_estimate=cost(10 * rows * width),
        name="add",
    )(lists, tile_counts, *pieces, *border_terms)
    return attended, grad_queries, grad_keys, grad_values


def solution(mesh):
    tokens = P(("clips", "tm", "ulysses"), None)
    return jax.shard_map(
        per_device,
        mesh=mesh,
        in_specs=(tokens, tokens, tokens, tokens, P("clips", None), P("clips")),
        out_specs=(tokens, tokens, tokens, tokens),
        check_vma=False,
    )
```

```python
import functools

import jax
import jax.numpy as jnp
from jax import lax
from jax.experimental import pallas as pl
from jax.experimental.pallas import tpu as pltpu
from jax.sharding import PartitionSpec as P

HEAD_DIM = 64
TILE = 64
FRAMES_SLAB = 2
PAIR = 2 * HEAD_DIM
BLOCK = 32
NEG = -1e30
VMEM_LIMIT = 24 * 1024 * 1024


class Plan:
    def __init__(self, rows, width, list_width):
        self.rows, self.width, self.list_width = rows, width, list_width
        self.slab = lax.axis_size("ulysses")
        self.slabs = lax.axis_size("tm")
        self.members = self.slab // FRAMES_SLAB
        self.frames = self.slabs * FRAMES_SLAB
        self.cols = width // self.members
        self.pairs = self.cols // PAIR
        self.device_tiles = rows // TILE
        self.frame_tiles = self.members * self.device_tiles
        self.remote = max(1, self.frame_tiles // 8)
        self.ext_tiles = self.frame_tiles + 2 * self.remote
        chunks = 2 if self.pairs % 2 == 0 else 1
        self.chunk_pairs = [self.pairs // chunks] * chunks
        self.span = 2 if self.chunk_pairs[0] % 2 == 0 else 1
        self.lanes = self.span * PAIR
        self.blocks = [count // self.span for count in self.chunk_pairs]
        self.unrolled = self.blocks[0] if self.frame_tiles <= 4 else 1
        self.whole_pieces = self.members == 2
        self.chunk_starts = [sum(self.chunk_pairs[:i]) for i in range(chunks)]

    def device(self, frame, member):
        place = frame % FRAMES_SLAB * self.members + member
        return place * self.slabs + frame // FRAMES_SLAB

    def member_perm(self, shift):
        return [
            (self.device(f, c), self.device(f, (c + shift) % self.members))
            for f in range(self.frames)
            for c in range(self.members)
        ]

    def frame_perm(self, far):
        pairs = [(f, partner(f, far)) for f in range(self.frames)]
        return [
            (self.device(f, c), self.device(other, c))
            for f, other in pairs
            if 0 <= other < self.frames
            for c in range(self.members)
        ]


def partner(frame, far):
    odd = frame % 2
    return frame - 1 + 2 * odd if far else frame + 1 - 2 * odd


def position(plan):
    place = lax.axis_index("ulysses")
    return lax.axis_index("tm") * FRAMES_SLAB + place // plan.members, place % plan.members


def piece_start(plan, me, offset):
    return pl.multiple_of(me * plan.cols + offset, PAIR) if plan.whole_pieces else offset


def listed(plan, lists_ref, counts_ref, reader, source):
    tiles = plan.frame_tiles
    row_start = jnp.clip(reader, 0, plan.frames - 1) * tiles
    base = source * tiles
    if plan.remote == 1:
        best = jnp.int32(0)
        for t in range(tiles):
            for j in range(plan.list_width):
                local = lists_ref[j, row_start + t] - base
                inside = (local >= 0) & (local < tiles) & (j < counts_ref[row_start + t])
                best = jnp.where(inside, local, best)
        return [best]

    def candidate(c, state):
        def row(t, found):
            for j in range(plan.list_width):
                hit = (lists_ref[j, row_start + t] == base + c) & (j < counts_ref[row_start + t])
                found = jnp.where(hit, 1, found)
            return found

        found = lax.fori_loop(0, tiles, row, jnp.int32(0))
        seen, picks = state
        picks = tuple(jnp.where((found == 1) & (seen == i), c, pick) for i, pick in enumerate(picks))
        return seen + found, picks

    start = (jnp.int32(0), tuple(jnp.int32(0) for _ in range(plan.remote)))
    return list(lax.fori_loop(0, tiles, candidate, start)[1])


def split_kernel(plan, *refs):
    count = (len(refs) - 1) // plan.members
    sources, outs, sem = refs[:count], refs[count:-1], refs[-1]
    _, me = position(plan)
    copies = []
    for r in range(1, plan.members):
        columns = pl.ds(pl.multiple_of((me + r) % plan.members * plan.cols, PAIR), plan.cols)
        for a, source in enumerate(sources):
            for row in range(0, plan.rows, BLOCK):
                rows = pl.ds(row, BLOCK)
                slot = len(copies)
                copies.append(
                    pltpu.make_async_copy(source.at[rows, columns], outs[(r - 1) * count + a].at[rows, :], sem.at[slot])
                )
    for copy in copies:
        copy.start()
    for copy in copies:
        copy.wait()


def slice_kernel(plan, after, *refs):
    refs = refs[after:]
    count = len(refs) // plan.members
    _, me = position(plan)
    for r in range(1, plan.members):
        columns = pl.ds(pl.multiple_of((me + r) % plan.members * plan.cols, PAIR), plan.cols)
        for a in range(count):
            refs[r * count + a][...] = refs[a][:, columns]


def pick_kernel(plan, g, lists_ref, counts_ref, *refs):
    members = plan.members
    own = refs[:2]
    pieces = refs[2 : 2 * members]
    outs = refs[-2:]
    frame, me = position(plan)
    cols = plan.chunk_pairs[g] * PAIR
    offset = plan.chunk_starts[g] * PAIR
    for far in range(2):
        picks = listed(plan, lists_ref, counts_ref, partner(frame, far), frame)
        for j, pick in enumerate(picks):
            owner = pick // plan.device_tiles
            row = pl.multiple_of(pick % plan.device_tiles * TILE, TILE)
            place = (me + members - owner) % members

            @pl.when(place == 0)
            def _():
                start = pl.multiple_of(me * plan.cols + offset, PAIR)
                for a in range(2):
                    outs[far][a, j] = own[a][pl.ds(row, TILE), pl.ds(start, cols)]

            for r in range(1, members):

                @pl.when(place == r)
                def _():
                    for a in range(2):
                        piece = pieces[(r - 1) * 2 + a]
                        outs[far][a, j] = piece[pl.ds(row, TILE), pl.ds(piece_start(plan, me, offset), cols)]


def attend_kernel(plan, g, lists_ref, counts_ref, *refs):
    members, tiles, remote, width = plan.members, plan.frame_tiles, plan.remote, plan.list_width
    per = plan.device_tiles
    others = members - 1
    own = refs[:4]
    key_value = refs[4 : 4 + 2 * others]
    query_grad = refs[4 + 2 * others : 4 + 4 * others]
    borders = refs[4 + 4 * others : 6 + 4 * others]
    rest = refs[6 + 4 * others :]
    earlier, rest = rest[: g * members], rest[g * members :]
    outs, parts = rest[:members], rest[members : members + 2]
    k_s, v_s, dk_s, dv_s, slots = rest[members + 2 :]
    last = g == len(plan.chunk_pairs) - 1
    for c in range(g if last else 0):
        done = pl.ds(plan.chunk_starts[c] * PAIR, plan.chunk_pairs[c] * PAIR)
        for r in range(members):
            outs[r][:, :, done] = earlier[c * members + r][...]
    frame, me = position(plan)
    partners = [partner(frame, far) for far in range(2)]
    known = [listed(plan, lists_ref, counts_ref, frame, other) for other in partners]
    live = []
    for t in range(tiles):
        row = frame * tiles + (me + members - t // per) % members * per + t % per
        live.append(counts_ref[row])
        for j in range(width):
            tile = lists_ref[j, row]
            local = tile - frame * tiles
            slot = (me + members - local // per) % members * per + local % per
            for far in range(2):
                local = tile - partners[far] * tiles
                rank = jnp.int32(0)
                for i in range(1, remote):
                    rank = jnp.where(local == known[far][i], i, rank)
                inside = (local >= 0) & (local < tiles)
                slot = jnp.where(inside, tiles + far * remote + rank, slot)
            slots[t, j] = slot

    lanes, heads = plan.lanes, plan.lanes // HEAD_DIM
    head_of = lax.broadcasted_iota(jnp.int32, (TILE, lanes), 1) // HEAD_DIM
    first = lax.broadcasted_iota(jnp.int32, (TILE, PAIR), 1) < HEAD_DIM
    scale = HEAD_DIM ** (-0.5)
    natural = (((1,), (0,)), ((), ()))
    inner = (((1,), (1,)), ((), ()))
    outer = (((0,), (0,)), ((), ()))

    def dot(left, right, dims):
        return lax.dot_general(left, right, dims, preferred_element_type=jnp.float32)

    def apart(rows):
        zero = jnp.zeros_like(rows)
        return jnp.concatenate([jnp.where(head_of == h, rows, zero) for h in range(heads)], axis=0)

    def together(terms, rows):
        pairs = []
        for s in range(plan.span):
            columns = slice(s * PAIR, (s + 1) * PAIR)
            both = dot(terms[:, columns], rows[:, columns], outer)
            pairs.append(jnp.where(first, both[:TILE], both[TILE:]))
        return jnp.concatenate(pairs, axis=1)

    def spans(p):
        offset = p * lanes
        start = plan.chunk_starts[g] * PAIR + offset
        if not isinstance(p, int):
            offset, start = pl.multiple_of(offset, lanes), pl.multiple_of(start, PAIR)
        here = pl.ds(pl.multiple_of(me * plan.cols + start, PAIR), lanes)
        there = pl.ds(piece_start(plan, me, start), lanes)
        span = pl.ds(offset, lanes)
        cut = pl.ds(start, lanes)
        return here, there, cut, span, cut if last else span

    def prepare(p, b):
        here, there, _, span, _ = spans(p)
        for a, scratch in enumerate((k_s, v_s)):
            for i in range(per):
                rows = pl.ds(i * TILE, TILE)
                scratch[b, i] = own[1 + a][rows, here]
                for r in range(1, members):
                    scratch[b, r * per + i] = key_value[(r - 1) * 2 + a][rows, there]
            for far in range(2):
                for i in range(remote):
                    scratch[b, tiles + far * remote + i] = borders[far][a, i, :, span]
        dk_s[b] = jnp.zeros(dk_s.shape[1:], dk_s.dtype)
        dv_s[b] = jnp.zeros(dv_s.shape[1:], dv_s.dtype)

    def first_products(p, b, t):
        here, _, cut, _, _ = spans(p)

        def load(a):
            rows = pl.ds(t % per * TILE, TILE)
            if t < per:
                return own[a][rows, here]
            return query_grad[(t // per - 1) * 2 + a // 3][rows, cut]

        at = [slots[t, j] for j in range(width)]
        queries = apart(load(0) * jnp.bfloat16(scale))
        grads = apart(load(3))
        keys = jnp.concatenate([k_s[b, s] for s in at], axis=0)
        values = jnp.concatenate([v_s[b, s] for s in at], axis=0)
        return at, queries, grads, keys, values, dot(keys, queries, inner), dot(values, grads, inner)

    def softmax(t, scores, grad_probs):
        masked = jnp.concatenate(
            [jnp.where(j < live[t], scores[j * TILE : (j + 1) * TILE], NEG) for j in range(width)], axis=0
        )
        terms = jnp.exp(masked - jnp.max(masked, axis=0, keepdims=True))
        probs = terms * (1.0 / jnp.sum(terms, axis=0, keepdims=True))
        delta = jnp.sum(probs * grad_probs, axis=0, keepdims=True)
        return probs.astype(jnp.bfloat16), (probs * (grad_probs - delta)).astype(jnp.bfloat16)

    def second_products(p, b, t, at, queries, grads, keys, values, probs_low, grad_low):
        result = spans(p)[-1]
        rows = pl.ds(t % per * TILE, TILE)
        out = outs[t // per]
        out[0, rows, result] = together(probs_low, values).astype(jnp.bfloat16)
        out[1, rows, result] = (together(grad_low, keys) * scale).astype(jnp.bfloat16)
        key_part = dot(grad_low, queries, natural)
        value_part = dot(probs_low, grads, natural)
        for j, s in enumerate(at):
            dk_s[b, s] += key_part[j * TILE : (j + 1) * TILE]
            dv_s[b, s] += value_part[j * TILE : (j + 1) * TILE]

    def finish(p, b):
        _, _, _, span, result = spans(p)
        for a, scratch in enumerate((dk_s, dv_s)):
            for t in range(tiles):
                rows = pl.ds(t % per * TILE, TILE)
                outs[t // per][2 + a, rows, result] = scratch[b, t].astype(jnp.bfloat16)
            for far in range(2):
                for i in range(remote):
                    parts[far][a, i, :, span] = scratch[b, tiles + far * remote + i].astype(jnp.bfloat16)

    def some_blocks(places):
        steps = [(p, b, t) for b, p in enumerate(places) for t in range(tiles)]
        products, weights = {}, {}
        for n in range(len(steps) + 2):
            if n < len(steps):
                p, b, t = steps[n]
                if t == 0:
                    prepare(p, b)
                products[n] = first_products(p, b, t)
            if 0 <= n - 1 < len(steps):
                weights[n - 1] = softmax(steps[n - 1][2], *products[n - 1][5:])
            if 0 <= n - 2:
                p, b, t = steps[n - 2]
                second_products(p, b, t, *products.pop(n - 2)[:5], *weights.pop(n - 2))
                if t == tiles - 1:
                    finish(p, b)

    if plan.unrolled == plan.blocks[g]:
        some_blocks(range(plan.blocks[g]))
    else:
        lax.fori_loop(0, plan.blocks[g], lambda p, carry: (some_blocks([p]), carry)[1], 0)


def write_out(scratch, outs, sem, fill):
    copies = []
    for a in range(2):
        for i in range(outs[a].shape[0] // TILE):
            rows = pl.ds(i * TILE, TILE)
            fill(a, i, rows)
            slot = len(copies)
            copies.append(pltpu.make_async_copy(scratch.at[a, rows, :], outs[a].at[rows, :], sem.at[slot]))
            copies[-1].start()
    for copy in copies:
        copy.wait()


def join_kernel(plan, *refs):
    members, outs, scratch, sem = plan.members, refs[-4:-2], refs[-2], refs[-1]
    _, me = position(plan)

    def fill(a, i, rows):
        for r in range(members):
            start = pl.multiple_of((me + r) % members * plan.cols, PAIR)
            scratch[a, rows, pl.ds(start, plan.cols)] = refs[r][a, rows, :]

    write_out(scratch, outs, sem, fill)


def add_kernel(plan, lists_ref, counts_ref, *refs):
    members, outs, scratch, sem = plan.members, refs[-4:-2], refs[-2], refs[-1]
    pieces, borders = refs[:members], refs[members:-4]
    frame, me = position(plan)
    partners = [partner(frame, far) for far in range(2)]
    picks = [listed(plan, lists_ref, counts_ref, other, frame) for other in partners]

    def fill(a, i, rows):
        hits = []
        for far in range(2):
            exists = (partners[far] >= 0) & (partners[far] < plan.frames)
            for j, pick in enumerate(picks[far]):
                hits.append((far, j, exists & (pick == me * plan.device_tiles + i)))
        for r in range(members):
            start = pl.multiple_of((me + r) % members * plan.cols, PAIR)
            scratch[a, rows, pl.ds(start, plan.cols)] = pieces[r][2 + a, rows, :]

        @pl.when(functools.reduce(lambda x, y: x | y, [hit for _, _, hit in hits]))
        def _():
            for g, count in enumerate(plan.chunk_pairs):
                for r in range(members):
                    columns = pl.ds(plan.chunk_starts[g] * PAIR, count * PAIR)
                    start = (me + r) % members * plan.cols + plan.chunk_starts[g] * PAIR
                    total = pieces[r][2 + a, rows, columns].astype(jnp.float32)
                    for far, j, hit in hits:
                        border = borders[(g * members + r) * 2 + 1 - far]
                        total += jnp.where(hit, border[a, j].astype(jnp.float32), 0.0)
                    span = pl.ds(pl.multiple_of(start, PAIR), count * PAIR)
                    scratch[a, rows, span] = total.astype(jnp.bfloat16)

    write_out(scratch, outs, sem, fill)


def per_device(queries, key_vectors, value_vectors, grad_out, key_tiles, tile_counts):
    rows, width = queries.shape
    plan = Plan(rows, width, key_tiles.shape[1])
    members, remote, chunks = plan.members, plan.remote, len(plan.chunk_pairs)
    axes = ("ulysses", "tm")
    lists = key_tiles.T
    low = jnp.bfloat16
    scalars = pl.BlockSpec(memory_space=pltpu.SMEM)
    whole = pl.BlockSpec(memory_space=pltpu.VMEM)
    anywhere = pl.BlockSpec(memory_space=pl.ANY)
    shape = jax.ShapeDtypeStruct
    params = pltpu.CompilerParams(vmem_limit_bytes=VMEM_LIMIT)

    def cost(moved, flops=0, terms=0):
        return pl.CostEstimate(flops=flops, bytes_accessed=moved, transcendentals=terms)

    def exchange(name, whole_rows, after, *sources):
        if plan.whole_pieces and whole_rows:
            return [lax.ppermute(x, axes, plan.member_perm(1)) for x in sources]
        places = (members - 1) * len(sources) * (rows // BLOCK)
        direct = not plan.whole_pieces
        after = [] if direct else after
        kernel = functools.partial(split_kernel, plan) if direct else functools.partial(slice_kernel, plan, len(after))
        sends = pl.pallas_call(
            kernel,
            out_shape=[shape((rows, plan.cols), low)] * (members - 1) * len(sources),
            in_specs=[anywhere] * len(after) + [anywhere if direct else whole] * len(sources),
            out_specs=[whole] * (members - 1) * len(sources),
            scratch_shapes=[pltpu.SemaphoreType.DMA((places,))] if direct else [],
            compiler_params=params,
            cost_estimate=cost(4 * len(sources) * rows * width),
            name=name,
        )(*after, *[pltpu.with_memory_space_constraint(x, pltpu.HBM) if direct else x for x in sources])
        each = len(sources)
        return [lax.ppermute(x, axes, plan.member_perm(1 + n // each)) for n, x in enumerate(sends)]

    key_value = exchange("split_kv", True, [], key_vectors, value_vectors)

    def hold_kernel(after, *refs):
        refs = refs[after:]
        for source, out in zip(refs[: len(refs) // 2], refs[len(refs) // 2 :], strict=True):
            out[...] = source[...]

    def hold(name, after, *sources):
        return pl.pallas_call(
            functools.partial(hold_kernel, len(after)),
            out_shape=[shape(x.shape, low) for x in sources],
            in_specs=[anywhere] * len(after) + [whole] * len(sources),
            out_specs=[whole] * len(sources),
            compiler_params=params,
            cost_estimate=cost(4 * sum(x.size for x in sources)),
            name=name,
        )(*after, *sources)

    arrived = []
    for g, count in enumerate(plan.chunk_pairs):
        picked = pl.pallas_call(
            functools.partial(pick_kernel, plan, g),
            out_shape=[shape((2, remote, TILE, count * PAIR), low)] * 2,
            in_specs=[scalars] * 2 + [whole] * (2 * members),
            out_specs=[whole] * 2,
            compiler_params=params,
            cost_estimate=cost(16 * remote * TILE * count * PAIR),
            name=f"pick_{g}",
        )(lists, tile_counts, key_vectors, value_vectors, *key_value)
        near, far = picked
        if g > 0:
            [near] = hold(f"hold_near_{g}", [arrived[-1][0]], near)
        arrived.append([lax.ppermute(x, axes, plan.frame_perm(i)) for i, x in enumerate((near, far))])
    query_grad = exchange("split_qg", False, [], queries, grad_out)

    def home(sent, r):
        return lax.ppermute(sent, axes, plan.member_perm(members - r))

    earlier, border_terms, nears, fars = [], [], [], []
    for g, count in enumerate(plan.chunk_pairs):
        cols = count * PAIR
        wide = plan.cols if g == chunks - 1 else cols
        scores = plan.frame_tiles * plan.list_width * TILE * 2 * TILE * count
        outs = pl.pallas_call(
            functools.partial(attend_kernel, plan, g),
            out_shape=[shape((4, rows, wide), low)] * members + [shape((2, remote, TILE, cols), low)] * 2,
            in_specs=[scalars] * 2 + [whole] * (4 + 4 * (members - 1) + 2 + len(earlier)),
            out_specs=[whole] * (members + 2),
            scratch_shapes=[
                pltpu.VMEM((plan.unrolled, plan.ext_tiles, TILE, plan.lanes), low),
                pltpu.VMEM((plan.unrolled, plan.ext_tiles, TILE, plan.lanes), low),
                pltpu.VMEM((plan.unrolled, plan.ext_tiles, TILE, plan.lanes), jnp.float32),
                pltpu.VMEM((plan.unrolled, plan.ext_tiles, TILE, plan.lanes), jnp.float32),
                pltpu.SMEM((plan.frame_tiles, plan.list_width), jnp.int32),
            ],
            compiler_params=params,
            cost_estimate=cost(16 * members * rows * cols, 12 * scores * PAIR, scores),
            name=f"attend_{g}",
        )(
            lists, tile_counts, queries, key_vectors, value_vectors, grad_out,
            *key_value, *query_grad, *arrived[g], *earlier,
        )
        parts = list(outs[members:])
        earlier += outs[:members]
        if g > 0:
            late = [parts[1], parts[0], *earlier[1 - members :]]
            parts[1], parts[0], *earlier[1 - members :] = hold(f"hold_{g}", [fars[-1], nears[-1]], *late)
        fars.append(lax.ppermute(parts[1], axes, plan.frame_perm(1)))
        nears.append(lax.ppermute(parts[0], axes, plan.frame_perm(0)))
    for near, far in zip(nears, fars, strict=True):
        border_terms += [far, near]
        for r in range(1, members):
            border_terms += [home(far, r), home(near, r)]
    pieces = [earlier[-members], *[home(earlier[r - members], r) for r in range(1, members)]]

    attended, grad_queries = pl.pallas_call(
        functools.partial(join_kernel, plan),
        out_shape=[shape((rows, width), low)] * 2,
        in_specs=[whole] * members,
        out_specs=[pl.BlockSpec(memory_space=pltpu.HBM)] * 2,
        scratch_shapes=[pltpu.VMEM((2, rows, width), low), pltpu.SemaphoreType.DMA((2 * plan.device_tiles,))],
        compiler_params=params,
        cost_estimate=cost(8 * rows * width),
        name="join",
    )(*pieces)
    grad_keys, grad_values = pl.pallas_call(
        functools.partial(add_kernel, plan),
        out_shape=[shape((rows, width), low)] * 2,
        in_specs=[scalars] * 2 + [whole] * (members + len(border_terms)),
        out_specs=[pl.BlockSpec(memory_space=pltpu.HBM)] * 2,
        scratch_shapes=[pltpu.VMEM((2, rows, width), low), pltpu.SemaphoreType.DMA((2 * plan.device_tiles,))],
        compiler_params=params,
        cost_estimate=cost(10 * rows * width),
        name="add",
    )(lists, tile_counts, *pieces, *border_terms)
    return attended, grad_queries, grad_keys, grad_values


def solution(mesh):
    tokens = P(("clips", "tm", "ulysses"), None)
    return jax.shard_map(
        per_device,
        mesh=mesh,
        in_specs=(tokens, tokens, tokens, tokens, P("clips", None), P("clips")),
        out_specs=(tokens, tokens, tokens, tokens),
        check_vma=False,
    )
```

```python
import functools

import jax
import jax.numpy as jnp
from jax import lax
from jax.experimental import pallas as pl
from jax.experimental.pallas import tpu as pltpu
from jax.sharding import PartitionSpec as P

HEAD_DIM = 64
TILE = 64
FRAMES_SLAB = 2
PAIR = 2 * HEAD_DIM
BLOCK = 32
NEG = -1e30
VMEM_LIMIT = 24 * 1024 * 1024


class Plan:
    def __init__(self, rows, width, list_width):
        self.rows, self.width, self.list_width = rows, width, list_width
        self.slab = lax.axis_size("ulysses")
        self.slabs = lax.axis_size("tm")
        self.members = self.slab // FRAMES_SLAB
        self.frames = self.slabs * FRAMES_SLAB
        self.cols = width // self.members
        self.pairs = self.cols // PAIR
        self.device_tiles = rows // TILE
        self.frame_tiles = self.members * self.device_tiles
        self.remote = max(1, self.frame_tiles // 8)
        self.ext_tiles = self.frame_tiles + 2 * self.remote
        chunks = 2 if self.pairs % 2 == 0 else 1
        self.chunk_pairs = [self.pairs // chunks] * chunks
        self.span = 2 if self.chunk_pairs[0] % 2 == 0 else 1
        self.lanes = self.span * PAIR
        self.blocks = [count // self.span for count in self.chunk_pairs]
        self.unrolled = self.blocks[0] if self.frame_tiles <= 4 else 1
        self.whole_pieces = self.members == 2
        self.chunk_starts = [sum(self.chunk_pairs[:i]) for i in range(chunks)]

    def device(self, frame, member):
        place = frame % FRAMES_SLAB * self.members + member
        return place * self.slabs + frame // FRAMES_SLAB

    def member_perm(self, shift):
        return [
            (self.device(f, c), self.device(f, (c + shift) % self.members))
            for f in range(self.frames)
            for c in range(self.members)
        ]

    def frame_perm(self, far):
        pairs = [(f, partner(f, far)) for f in range(self.frames)]
        return [
            (self.device(f, c), self.device(other, c))
            for f, other in pairs
            if 0 <= other < self.frames
            for c in range(self.members)
        ]


def partner(frame, far):
    odd = frame % 2
    return frame - 1 + 2 * odd if far else frame + 1 - 2 * odd


def position(plan):
    place = lax.axis_index("ulysses")
    return lax.axis_index("tm") * FRAMES_SLAB + place // plan.members, place % plan.members


def piece_start(plan, me, offset):
    return pl.multiple_of(me * plan.cols + offset, PAIR) if plan.whole_pieces else offset


def listed(plan, lists_ref, counts_ref, reader, source):
    tiles = plan.frame_tiles
    row_start = jnp.clip(reader, 0, plan.frames - 1) * tiles
    base = source * tiles
    if plan.remote == 1:
        best = jnp.int32(0)
        for t in range(tiles):
            for j in range(plan.list_width):
                local = lists_ref[j, row_start + t] - base
                inside = (local >= 0) & (local < tiles) & (j < counts_ref[row_start + t])
                best = jnp.where(inside, local, best)
        return [best]

    def candidate(c, state):
        def row(t, found):
            for j in range(plan.list_width):
                hit = (lists_ref[j, row_start + t] == base + c) & (j < counts_ref[row_start + t])
                found = jnp.where(hit, 1, found)
            return found

        found = lax.fori_loop(0, tiles, row, jnp.int32(0))
        seen, picks = state
        picks = tuple(jnp.where((found == 1) & (seen == i), c, pick) for i, pick in enumerate(picks))
        return seen + found, picks

    start = (jnp.int32(0), tuple(jnp.int32(0) for _ in range(plan.remote)))
    return list(lax.fori_loop(0, tiles, candidate, start)[1])


def split_kernel(plan, *refs):
    count = (len(refs) - 1) // plan.members
    sources, outs, sem = refs[:count], refs[count:-1], refs[-1]
    _, me = position(plan)
    copies = []
    for r in range(1, plan.members):
        columns = pl.ds(pl.multiple_of((me + r) % plan.members * plan.cols, PAIR), plan.cols)
        for a, source in enumerate(sources):
            for row in range(0, plan.rows, BLOCK):
                rows = pl.ds(row, BLOCK)
                slot = len(copies)
                copies.append(
                    pltpu.make_async_copy(source.at[rows, columns], outs[(r - 1) * count + a].at[rows, :], sem.at[slot])
                )
    for copy in copies:
        copy.start()
    for copy in copies:
        copy.wait()


def slice_kernel(plan, after, *refs):
    refs = refs[after:]
    count = len(refs) // plan.members
    _, me = position(plan)
    for r in range(1, plan.members):
        columns = pl.ds(pl.multiple_of((me + r) % plan.members * plan.cols, PAIR), plan.cols)
        for a in range(count):
            refs[r * count + a][...] = refs[a][:, columns]


def pick_kernel(plan, g, lists_ref, counts_ref, *refs):
    members = plan.members
    own = refs[:2]
    pieces = refs[2 : 2 * members]
    outs = refs[-2:]
    frame, me = position(plan)
    cols = plan.chunk_pairs[g] * PAIR
    offset = plan.chunk_starts[g] * PAIR
    for far in range(2):
        picks = listed(plan, lists_ref, counts_ref, partner(frame, far), frame)
        for j, pick in enumerate(picks):
            owner = pick // plan.device_tiles
            row = pl.multiple_of(pick % plan.device_tiles * TILE, TILE)
            place = (me + members - owner) % members

            @pl.when(place == 0)
            def _():
                start = pl.multiple_of(me * plan.cols + offset, PAIR)
                for a in range(2):
                    outs[far][a, j] = own[a][pl.ds(row, TILE), pl.ds(start, cols)]

            for r in range(1, members):

                @pl.when(place == r)
                def _():
                    for a in range(2):
                        piece = pieces[(r - 1) * 2 + a]
                        outs[far][a, j] = piece[pl.ds(row, TILE), pl.ds(piece_start(plan, me, offset), cols)]


def attend_kernel(plan, g, lists_ref, counts_ref, *refs):
    members, tiles, remote, width = plan.members, plan.frame_tiles, plan.remote, plan.list_width
    per = plan.device_tiles
    others = members - 1
    own = refs[:4]
    key_value = refs[4 : 4 + 2 * others]
    query_grad = refs[4 + 2 * others : 4 + 4 * others]
    borders = refs[4 + 4 * others : 6 + 4 * others]
    rest = refs[6 + 4 * others :]
    earlier, rest = rest[: g * members], rest[g * members :]
    outs, parts = rest[:members], rest[members : members + 2]
    k_s, v_s, dk_s, dv_s, slots = rest[members + 2 :]
    last = g == len(plan.chunk_pairs) - 1
    for c in range(g if last else 0):
        done = pl.ds(plan.chunk_starts[c] * PAIR, plan.chunk_pairs[c] * PAIR)
        for r in range(members):
            outs[r][:, :, done] = earlier[c * members + r][...]
    frame, me = position(plan)
    partners = [partner(frame, far) for far in range(2)]
    known = [listed(plan, lists_ref, counts_ref, frame, other) for other in partners]
    live = []
    for t in range(tiles):
        row = frame * tiles + (me + members - t // per) % members * per + t % per
        live.append(counts_ref[row])
        for j in range(width):
            tile = lists_ref[j, row]
            local = tile - frame * tiles
            slot = (me + members - local // per) % members * per + local % per
            for far in range(2):
                local = tile - partners[far] * tiles
                rank = jnp.int32(0)
                for i in range(1, remote):
                    rank = jnp.where(local == known[far][i], i, rank)
                inside = (local >= 0) & (local < tiles)
                slot = jnp.where(inside, tiles + far * remote + rank, slot)
            slots[t, j] = slot

    lanes, heads = plan.lanes, plan.lanes // HEAD_DIM
    head_of = lax.broadcasted_iota(jnp.int32, (TILE, lanes), 1) // HEAD_DIM
    first = lax.broadcasted_iota(jnp.int32, (TILE, PAIR), 1) < HEAD_DIM
    scale = HEAD_DIM ** (-0.5)
    natural = (((1,), (0,)), ((), ()))
    inner = (((1,), (1,)), ((), ()))
    outer = (((0,), (0,)), ((), ()))

    def dot(left, right, dims):
        return lax.dot_general(left, right, dims, preferred_element_type=jnp.float32)

    def apart(rows):
        zero = jnp.zeros_like(rows)
        return jnp.concatenate([jnp.where(head_of == h, rows, zero) for h in range(heads)], axis=0)

    def together(terms, rows):
        pairs = []
        for s in range(plan.span):
            columns = slice(s * PAIR, (s + 1) * PAIR)
            both = dot(terms[:, columns], rows[:, columns], outer)
            pairs.append(jnp.where(first, both[:TILE], both[TILE:]))
        return jnp.concatenate(pairs, axis=1)

    def spans(p):
        offset = p * lanes
        start = plan.chunk_starts[g] * PAIR + offset
        if not isinstance(p, int):
            offset, start = pl.multiple_of(offset, lanes), pl.multiple_of(start, PAIR)
        here = pl.ds(pl.multiple_of(me * plan.cols + start, PAIR), lanes)
        there = pl.ds(piece_start(plan, me, start), lanes)
        span = pl.ds(offset, lanes)
        cut = pl.ds(start, lanes)
        return here, there, cut, span, cut if last else span

    def prepare(p, b):
        here, there, _, span, _ = spans(p)
        for a, scratch in enumerate((k_s, v_s)):
            for i in range(per):
                rows = pl.ds(i * TILE, TILE)
                scratch[b, i] = own[1 + a][rows, here]
                for r in range(1, members):
                    scratch[b, r * per + i] = key_value[(r - 1) * 2 + a][rows, there]
            for far in range(2):
                for i in range(remote):
                    scratch[b, tiles + far * remote + i] = borders[far][a, i, :, span]
        dk_s[b] = jnp.zeros(dk_s.shape[1:], dk_s.dtype)
        dv_s[b] = jnp.zeros(dv_s.shape[1:], dv_s.dtype)

    def first_products(p, b, t):
        here, _, cut, _, _ = spans(p)

        def load(a):
            rows = pl.ds(t % per * TILE, TILE)
            if t < per:
                return own[a][rows, here]
            return query_grad[(t // per - 1) * 2 + a // 3][rows, cut]

        at = [slots[t, j] for j in range(width)]
        queries = apart(load(0) * jnp.bfloat16(scale))
        grads = apart(load(3))
        keys = jnp.concatenate([k_s[b, s] for s in at], axis=0)
        values = jnp.concatenate([v_s[b, s] for s in at], axis=0)
        return at, queries, grads, keys, values, dot(keys, queries, inner), dot(values, grads, inner)

    def softmax(t, scores, grad_probs):
        masked = jnp.concatenate(
            [jnp.where(j < live[t], scores[j * TILE : (j + 1) * TILE], NEG) for j in range(width)], axis=0
        )
        terms = jnp.exp(masked - jnp.max(masked, axis=0, keepdims=True))
        probs = terms * (1.0 / jnp.sum(terms, axis=0, keepdims=True))
        delta = jnp.sum(probs * grad_probs, axis=0, keepdims=True)
        return probs.astype(jnp.bfloat16), (probs * (grad_probs - delta)).astype(jnp.bfloat16)

    def second_products(p, b, t, at, queries, grads, keys, values, probs_low, grad_low):
        result = spans(p)[-1]
        rows = pl.ds(t % per * TILE, TILE)
        out = outs[t // per]
        out[0, rows, result] = together(probs_low, values).astype(jnp.bfloat16)
        out[1, rows, result] = (together(grad_low, keys) * scale).astype(jnp.bfloat16)
        key_part = dot(grad_low, queries, natural)
        value_part = dot(probs_low, grads, natural)
        for j, s in enumerate(at):
            dk_s[b, s] += key_part[j * TILE : (j + 1) * TILE]
            dv_s[b, s] += value_part[j * TILE : (j + 1) * TILE]

    def finish(p, b):
        _, _, _, span, result = spans(p)
        for a, scratch in enumerate((dk_s, dv_s)):
            for t in range(tiles):
                rows = pl.ds(t % per * TILE, TILE)
                outs[t // per][2 + a, rows, result] = scratch[b, t].astype(jnp.bfloat16)
            for far in range(2):
                for i in range(remote):
                    parts[far][a, i, :, span] = scratch[b, tiles + far * remote + i].astype(jnp.bfloat16)

    def some_blocks(places):
        steps = [(p, b, t) for b, p in enumerate(places) for t in range(tiles)]
        products, weights = {}, {}
        for n in range(len(steps) + 2):
            if n < len(steps):
                p, b, t = steps[n]
                if t == 0:
                    prepare(p, b)
                products[n] = first_products(p, b, t)
            if 0 <= n - 1 < len(steps):
                weights[n - 1] = softmax(steps[n - 1][2], *products[n - 1][5:])
            if 0 <= n - 2:
                p, b, t = steps[n - 2]
                second_products(p, b, t, *products.pop(n - 2)[:5], *weights.pop(n - 2))
                if t == tiles - 1:
                    finish(p, b)

    if plan.unrolled == plan.blocks[g]:
        some_blocks(range(plan.blocks[g]))
    else:
        lax.fori_loop(0, plan.blocks[g], lambda p, carry: (some_blocks([p]), carry)[1], 0)


def write_out(scratch, outs, sem, fill):
    copies = []
    for a in range(2):
        for i in range(outs[a].shape[0] // TILE):
            rows = pl.ds(i * TILE, TILE)
            fill(a, i, rows)
            slot = len(copies)
            copies.append(pltpu.make_async_copy(scratch.at[a, rows, :], outs[a].at[rows, :], sem.at[slot]))
            copies[-1].start()
    for copy in copies:
        copy.wait()


def join_kernel(plan, *refs):
    members, outs, scratch, sem = plan.members, refs[-4:-2], refs[-2], refs[-1]
    _, me = position(plan)

    def fill(a, i, rows):
        for r in range(members):
            start = pl.multiple_of((me + r) % members * plan.cols, PAIR)
            scratch[a, rows, pl.ds(start, plan.cols)] = refs[r][a, rows, :]

    write_out(scratch, outs, sem, fill)


def touching(plan, lists_ref, counts_ref):
    frame, me = position(plan)
    partners = [partner(frame, far) for far in range(2)]
    picks = [listed(plan, lists_ref, counts_ref, other, frame) for other in partners]

    def hits(i):
        found = []
        for far in range(2):
            exists = (partners[far] >= 0) & (partners[far] < plan.frames)
            for j, pick in enumerate(picks[far]):
                found.append((far, j, exists & (pick == me * plan.device_tiles + i)))
        return found, functools.reduce(lambda x, y: x | y, [hit for _, _, hit in found])

    return me, hits


def summed(plan, g, a, rows, piece, borders, found):
    columns = pl.ds(plan.chunk_starts[g] * PAIR, plan.chunk_pairs[g] * PAIR)
    total = piece[2 + a, rows, columns].astype(jnp.float32)
    for far, j, hit in found:
        total += jnp.where(hit, borders[far][a, j].astype(jnp.float32), 0.0)
    return total.astype(jnp.bfloat16)


def add_kernel(plan, lists_ref, counts_ref, *refs):
    members, outs, scratch, sem = plan.members, refs[-4:-2], refs[-2], refs[-1]
    pieces, borders = refs[:members], refs[members:-4]
    me, hits = touching(plan, lists_ref, counts_ref)

    def fill(a, i, rows):
        found, touched = hits(i)
        for r in range(members):
            start = pl.multiple_of((me + r) % members * plan.cols, PAIR)
            scratch[a, rows, pl.ds(start, plan.cols)] = pieces[r][2 + a, rows, :]

        @pl.when(touched)
        def _():
            for r in range(members):
                span = pl.ds(pl.multiple_of((me + r) % members * plan.cols, PAIR), plan.chunk_pairs[0] * PAIR)
                scratch[a, rows, span] = summed(plan, 0, a, rows, pieces[r], borders[2 * r : 2 * r + 2], found)

    write_out(scratch, outs, sem, fill)


def patch_kernel(plan, lists_ref, counts_ref, *refs):
    members, outs, scratch, sem = plan.members, refs[-4:-2], refs[-2], refs[-1]
    pieces, borders = refs[:members], refs[members : 3 * members]
    me, hits = touching(plan, lists_ref, counts_ref)
    cols = plan.chunk_pairs[1] * PAIR

    def copy(a, i, r):
        start = (me + r) % members * plan.cols + plan.chunk_starts[1] * PAIR
        target = outs[a].at[pl.ds(i * TILE, TILE), pl.ds(pl.multiple_of(start, PAIR), cols)]
        slot = (a * plan.device_tiles + i) * members + r
        return pltpu.make_async_copy(scratch.at[slot], target, sem.at[slot])

    places = [(a, i, r) for i in range(plan.device_tiles) for a in range(2) for r in range(members)]
    for a, i, r in places:
        found, touched = hits(i)

        @pl.when(touched)
        def _():
            rows = pl.ds(i * TILE, TILE)
            slot = (a * plan.device_tiles + i) * members + r
            scratch[slot] = summed(plan, 1, a, rows, pieces[r], borders[2 * r : 2 * r + 2], found)
            copy(a, i, r).start()

    for a, i, r in places:

        @pl.when(hits(i)[1])
        def _():
            copy(a, i, r).wait()


def per_device(queries, key_vectors, value_vectors, grad_out, key_tiles, tile_counts):
    rows, width = queries.shape
    plan = Plan(rows, width, key_tiles.shape[1])
    members, remote, chunks = plan.members, plan.remote, len(plan.chunk_pairs)
    axes = ("ulysses", "tm")
    lists = key_tiles.T
    low = jnp.bfloat16
    scalars = pl.BlockSpec(memory_space=pltpu.SMEM)
    whole = pl.BlockSpec(memory_space=pltpu.VMEM)
    anywhere = pl.BlockSpec(memory_space=pl.ANY)
    shape = jax.ShapeDtypeStruct
    params = pltpu.CompilerParams(vmem_limit_bytes=VMEM_LIMIT)

    def cost(moved, flops=0, terms=0):
        return pl.CostEstimate(flops=flops, bytes_accessed=moved, transcendentals=terms)

    def exchange(name, whole_rows, after, *sources):
        if plan.whole_pieces and whole_rows:
            return [lax.ppermute(x, axes, plan.member_perm(1)) for x in sources]
        places = (members - 1) * len(sources) * (rows // BLOCK)
        direct = not plan.whole_pieces
        after = [] if direct else after
        kernel = functools.partial(split_kernel, plan) if direct else functools.partial(slice_kernel, plan, len(after))
        sends = pl.pallas_call(
            kernel,
            out_shape=[shape((rows, plan.cols), low)] * (members - 1) * len(sources),
            in_specs=[anywhere] * len(after) + [anywhere if direct else whole] * len(sources),
            out_specs=[whole] * (members - 1) * len(sources),
            scratch_shapes=[pltpu.SemaphoreType.DMA((places,))] if direct else [],
            compiler_params=params,
            cost_estimate=cost(4 * len(sources) * rows * width),
            name=name,
        )(*after, *[pltpu.with_memory_space_constraint(x, pltpu.HBM) if direct else x for x in sources])
        each = len(sources)
        return [lax.ppermute(x, axes, plan.member_perm(1 + n // each)) for n, x in enumerate(sends)]

    key_value = exchange("split_kv", True, [], key_vectors, value_vectors)

    def hold_kernel(after, *refs):
        refs = refs[after:]
        for source, out in zip(refs[: len(refs) // 2], refs[len(refs) // 2 :], strict=True):
            out[...] = source[...]

    def hold(name, after, *sources):
        return pl.pallas_call(
            functools.partial(hold_kernel, len(after)),
            out_shape=[shape(x.shape, low) for x in sources],
            in_specs=[anywhere] * len(after) + [whole] * len(sources),
            out_specs=[whole] * len(sources),
            compiler_params=params,
            cost_estimate=cost(4 * sum(x.size for x in sources)),
            name=name,
        )(*after, *sources)

    arrived = []
    for g, count in enumerate(plan.chunk_pairs):
        picked = pl.pallas_call(
            functools.partial(pick_kernel, plan, g),
            out_shape=[shape((2, remote, TILE, count * PAIR), low)] * 2,
            in_specs=[scalars] * 2 + [whole] * (2 * members),
            out_specs=[whole] * 2,
            compiler_params=params,
            cost_estimate=cost(16 * remote * TILE * count * PAIR),
            name=f"pick_{g}",
        )(lists, tile_counts, key_vectors, value_vectors, *key_value)
        near, far = picked
        if g > 0:
            [near] = hold(f"hold_near_{g}", [arrived[-1][0]], near)
        arrived.append([lax.ppermute(x, axes, plan.frame_perm(i)) for i, x in enumerate((near, far))])
    query_grad = exchange("split_qg", False, [], queries, grad_out)

    def home(sent, r):
        return lax.ppermute(sent, axes, plan.member_perm(members - r))

    earlier, nears, fars = [], [], []
    for g, count in enumerate(plan.chunk_pairs):
        cols = count * PAIR
        wide = plan.cols if g == chunks - 1 else cols
        scores = plan.frame_tiles * plan.list_width * TILE * 2 * TILE * count
        outs = pl.pallas_call(
            functools.partial(attend_kernel, plan, g),
            out_shape=[shape((4, rows, wide), low)] * members + [shape((2, remote, TILE, cols), low)] * 2,
            in_specs=[scalars] * 2 + [whole] * (4 + 4 * (members - 1) + 2 + len(earlier)),
            out_specs=[whole] * (members + 2),
            scratch_shapes=[
                pltpu.VMEM((plan.unrolled, plan.ext_tiles, TILE, plan.lanes), low),
                pltpu.VMEM((plan.unrolled, plan.ext_tiles, TILE, plan.lanes), low),
                pltpu.VMEM((plan.unrolled, plan.ext_tiles, TILE, plan.lanes), jnp.float32),
                pltpu.VMEM((plan.unrolled, plan.ext_tiles, TILE, plan.lanes), jnp.float32),
                pltpu.SMEM((plan.frame_tiles, plan.list_width), jnp.int32),
            ],
            compiler_params=params,
            cost_estimate=cost(16 * members * rows * cols, 12 * scores * PAIR, scores),
            name=f"attend_{g}",
        )(
            lists, tile_counts, queries, key_vectors, value_vectors, grad_out,
            *key_value, *query_grad, *arrived[g], *earlier,
        )
        parts = list(outs[members:])
        earlier += outs[:members]
        if g > 0:
            held = hold(f"hold_far_{g}", [nears[-1], fars[-1]], parts[1], *earlier[1 - members :])
            parts[1], earlier[1 - members :] = held[0], held[1:]
        nears.append(lax.ppermute(parts[0], axes, plan.frame_perm(0)))
        fars.append(lax.ppermute(parts[1], axes, plan.frame_perm(1)))
    def everyone(near, far):
        return [near, far] + [home(x, r) for r in range(1, members) for x in (near, far)]

    pieces = [earlier[-members], *[home(earlier[r - members], r) for r in range(1, members)]]

    attended, grad_queries = pl.pallas_call(
        functools.partial(join_kernel, plan),
        out_shape=[shape((rows, width), low)] * 2,
        in_specs=[whole] * members,
        out_specs=[pl.BlockSpec(memory_space=pltpu.HBM)] * 2,
        scratch_shapes=[pltpu.VMEM((2, rows, width), low), pltpu.SemaphoreType.DMA((2 * plan.device_tiles,))],
        compiler_params=params,
        cost_estimate=cost(8 * rows * width),
        name="join",
    )(*pieces)
    in_hbm = pl.BlockSpec(memory_space=pltpu.HBM)
    gradients = pl.pallas_call(
        functools.partial(add_kernel, plan),
        out_shape=[shape((rows, width), low)] * 2,
        in_specs=[scalars] * 2 + [whole] * (3 * members),
        out_specs=[in_hbm] * 2,
        scratch_shapes=[pltpu.VMEM((2, rows, width), low), pltpu.SemaphoreType.DMA((2 * plan.device_tiles,))],
        compiler_params=params,
        cost_estimate=cost(20 * rows * width),
        name="add",
    )(lists, tile_counts, *pieces, *everyone(nears[0], fars[0]))
    if chunks > 1:
        places = 2 * plan.device_tiles * members
        written = [pltpu.with_memory_space_constraint(x, pltpu.HBM) for x in (attended, gradients[0])]
        late = hold("hold_last", written, nears[1], fars[1])
        gradients = pl.pallas_call(
            functools.partial(patch_kernel, plan),
            out_shape=[shape((rows, width), low)] * 2,
            in_specs=[scalars] * 2 + [whole] * (3 * members) + [in_hbm] * 2,
            out_specs=[in_hbm] * 2,
            scratch_shapes=[
                pltpu.VMEM((places, TILE, plan.chunk_pairs[1] * PAIR), low),
                pltpu.SemaphoreType.DMA((places,)),
            ],
            input_output_aliases={2 + 3 * members: 0, 3 + 3 * members: 1},
            compiler_params=params,
            cost_estimate=cost(4 * rows * width),
            name="patch",
        )(lists, tile_counts, *pieces, *everyone(*late), *gradients)
    grad_keys, grad_values = gradients
    return attended, grad_queries, grad_keys, grad_values


def solution(mesh):
    tokens = P(("clips", "tm", "ulysses"), None)
    return jax.shard_map(
        per_device,
        mesh=mesh,
        in_specs=(tokens, tokens, tokens, tokens, P("clips", None), P("clips")),
        out_specs=(tokens, tokens, tokens, tokens),
        check_vma=False,
    )
```
